32 devices in a mesh: group: 2 (over y), out: 4 (over z), inp: 2 (over x), dp: 2 (over core).
Axes of the slice: x: 2, y: 2, z: 4, core: 2. Of those that a mesh axis runs over, the one named last changes fastest.
Arguments:
- activations: bfloat16 [16, 128, 8192], P(('group', 'dp'), 'out', 'inp'), parts along dimension 0, may hold values from -6 to 6
- out_grads: bfloat16 [16, 128, 28672], P(('group', 'dp'), 'inp', 'out'), parts along dimension 0, may hold values from -6 to 6
- basis_in: bfloat16 [8192, 4096], P('inp', 'out'), may hold values from -0.0625 to 0.0625
- basis_out: bfloat16 [28672, 14336], P('out', ('inp', 'dp')), may hold values from -0.03125 to 0.03125
Outputs:
- eigenvalues: float32 [8192, 14336], P(('group', 'out'), ('inp', 'dp')), parts along dimension 0
The draws below stay inside these ranges and needn't reach their ends.
There are 2 independent parts, one for each index of `group`. The reference program is written for one: setup_inputs(seed, part) draws one part's arguments, and reference() takes and returns one part's arrays. A program takes and returns all parts, laid end to end along the dimension named above; an argument that names none is the same for every part. Nothing has to cross between parts.
All inputs are finite; a program needn't handle non-finite values.
Results may differ from the reference program's by a relative error of at most 0.0028.
Values may be sent and summed in bfloat16 or wider, within the bound.
A program may use at most 256 MiB of HBM per device.

```python
import jax
import jax.numpy as jnp
from jax import lax

D = 8192
F = 28672
DW = 4096
FW = 14336
TOK = 128
EX = 8


def shard_levels(stream_key, extent, cuts, low, largest):
    loudness, own = 1.0, jax.random.fold_in(stream_key, 6)
    for axis_at, shards_of in cuts:
        steps = jnp.exp(jax.random.uniform(jax.random.fold_in(own, axis_at), (shards_of,), jnp.float32, low / len(cuts), largest / len(cuts)))
        loudness = loudness * jnp.repeat(steps, extent[axis_at] // shards_of).reshape([-1 if axis == axis_at else 1 for axis in range(len(extent))])
    return loudness


def gaussian(key, shape, spread, reach, pieces=(), kind=jnp.bfloat16):
    entries = jax.random.normal(key, shape, jnp.float32) * spread
    if len(pieces) > 0:
        entries = shard_levels(key, shape, pieces, -0.22, 0.18) * entries
    return jnp.clip(entries, min=-reach, max=reach).astype(kind)


def setup_inputs(seed: int = 0, part: int = 0) -> dict:
    key_of = jax.random.split(jax.random.key(seed), 5)
    part_keys = jax.random.split(jax.random.fold_in(key_of[4], part), 5)
    return {
        "activations": gaussian(part_keys[0], (EX, TOK, D), 1.0, 6.0, ((0, 2), (1, 4), (2, 2))),
        "out_grads": gaussian(part_keys[1], (EX, TOK, F), 1.0, 6.0, ((0, 2), (1, 2), (2, 4))),
        "basis_in": gaussian(key_of[2], (D, DW), D ** -0.5, 0.0625, ((0, 2), (1, 4))),
        "basis_out": gaussian(key_of[3], (F, FW), F ** -0.5, 0.03125, ((0, 4), (1, 4))),
    }


def reference(activations, out_grads, basis_in, basis_out):
    examples, tokens, width = activations.shape
    hidden = out_grads.shape[2]
    act_hat = jnp.dot(activations.reshape(examples * tokens, width), basis_in, preferred_element_type=jnp.float32)
    act_hat = act_hat.astype(jnp.bfloat16).reshape(examples, tokens, DW)
    grad_hat = jnp.dot(out_grads.reshape(examples * tokens, hidden), basis_out, preferred_element_type=jnp.float32)
    grad_hat = grad_hat.astype(jnp.bfloat16).reshape(examples, tokens, FW)

    def accumulate(total, pair):
        act_one, grad_one = pair
        rotated = jnp.dot(act_one.T, grad_one, preferred_element_type=jnp.float32)
        return total + rotated * rotated, None

    total, unused = lax.scan(accumulate, jnp.zeros((DW, FW), jnp.float32), (act_hat, grad_hat))
    return total / (examples * tokens)
```

```python
import jax
import jax.numpy as jnp
from jax import lax
from jax.sharding import PartitionSpec as P

BF16 = jnp.bfloat16
F32 = jnp.float32


def sum_on_line(partial, axis, n):
    if n == 1:
        return partial.astype(BF16)
    if n % 2:
        return lax.psum(partial, axis).astype(BF16)
    me = lax.axis_index(axis)
    half = n // 2
    total = partial
    for step in range(half - 1):
        hops = [(step, step + 1), (n - 1 - step, n - 2 - step)]
        total = total + lax.ppermute(total.astype(BF16), axis, hops).astype(F32)
    swap = [(half - 1, half), (half, half - 1)]
    total = total + lax.ppermute(total.astype(BF16), axis, swap).astype(F32)
    out = total.astype(BF16)
    for step in range(half - 1):
        hops = [(half - 1 - step, half - 2 - step), (half + step, half + step + 1)]
        got = lax.ppermute(out, axis, hops)
        mine = (me == half - 2 - step) | (me == half + step + 1)
        out = jnp.where(mine, got, out)
    return out


def gather_on_line(block, axis, n):
    up = [(i, i + 1) for i in range(n - 1)]
    down = [(i + 1, i) for i in range(n - 1)]
    rights, lefts = [block], [block]
    for _ in range(n - 1):
        rights.append(lax.ppermute(rights[-1], axis, up))
        lefts.append(lax.ppermute(lefts[-1], axis, down))
    me = lax.axis_index(axis)
    slots = [block]
    for k in range(1, n):
        slots.append(jnp.where(me >= k, rights[k], lefts[n - k]))
    return slots


def make_body(n_out, n_inp, n_dp):
    def swap_dp(x):
        return lax.ppermute(x, "dp", [(0, 1), (1, 0)])

    def by_dp(mine, other):
        first = lax.axis_index("dp") == 0
        return jnp.concatenate([jnp.where(first, mine, other), jnp.where(first, other, mine)], axis=0)

    def in_order(slots, axis, n):
        me = lax.axis_index(axis)
        if n == 2:
            first = me == 0
            return [jnp.where(first, slots[0], slots[1]), jnp.where(first, slots[1], slots[0])]
        stacked = jnp.stack(slots)
        return [lax.dynamic_index_in_dim(stacked, lax.rem(me - j + n, n), 0, keepdims=False) for j in range(n)]

    def body(activations, out_grads, basis_in, basis_out):
        ex, tok, width = activations.shape
        grads = [out_grads]
        for k in range(1, n_inp):
            grads.append(lax.ppermute(out_grads, "inp", [(i, (i + k) % n_inp) for i in range(n_inp)]))
        acts = jnp.stack(gather_on_line(activations, "out", n_out))

        def project(block):
            e, t, f = block.shape
            partial = jnp.dot(block.reshape(e * t, f), basis_out, preferred_element_type=F32)
            cuts = 2 if e % 2 == 0 and (e // 2) * t % 16 == 0 else 1
            rows = e * t // cuts
            sums = [sum_on_line(partial[c * rows:(c + 1) * rows], "out", n_out) for c in range(cuts)]
            return jnp.concatenate(sums, axis=0).reshape(e, t, -1)

        mine, others = [], []
        for block in grads:
            mine.append(project(block))
            others.append(project(swap_dp(block)))

        act_partial = jnp.dot(acts.reshape(n_out * ex * tok, width), basis_in, preferred_element_type=F32)
        total = act_partial
        sent = act_partial.astype(BF16)
        for k in range(1, n_inp):
            total = total + lax.ppermute(sent, "inp", [(i, (i + k) % n_inp) for i in range(n_inp)]).astype(F32)
        act_own = total.astype(BF16).reshape(n_out, ex, tok, -1)
        act_own = jnp.concatenate(in_order([act_own[k] for k in range(n_out)], "out", n_out), axis=1)
        act_hat = by_dp(act_own, swap_dp(act_own))

        grad_mine = jnp.concatenate(in_order(mine, "inp", n_inp), axis=1)
        grad_others = jnp.concatenate(in_order(others, "inp", n_inp), axis=1)
        grad_hat = by_dp(grad_mine, grad_others)

        rotated = jnp.einsum("etd,etf->edf", act_hat, grad_hat, preferred_element_type=F32)
        count_rows = act_hat.shape[0] * act_hat.shape[1]
        return jnp.sum(rotated * rotated, axis=0) / count_rows

    return body


def solution(mesh):
    shape = dict(mesh.shape)
    placed = (
        P(("group", "dp"), "out", "inp"),
        P(("group", "dp"), "inp", "out"),
        P("inp", "out"),
        P("out", ("inp", "dp")),
    )
    return jax.shard_map(
        make_body(shape["out"], shape["inp"], shape["dp"]),
        mesh=mesh,
        in_specs=placed,
        out_specs=P(("group", "out"), ("inp", "dp")),
        check_vma=False,
    )
```

```python
import jax
import jax.numpy as jnp
from jax import lax
from jax.sharding import PartitionSpec as P

BF16 = jnp.bfloat16
F32 = jnp.float32


def sum_on_line(partial, axis, n):
    if n == 1:
        return partial.astype(BF16)
    if n % 2:
        return lax.psum(partial, axis).astype(BF16)
    me = lax.axis_index(axis)
    half = n // 2
    total = partial
    for step in range(half - 1):
        hops = [(step, step + 1), (n - 1 - step, n - 2 - step)]
        total = total + lax.ppermute(total.astype(BF16), axis, hops).astype(F32)
    swap = [(half - 1, half), (half, half - 1)]
    total = total + lax.ppermute(total.astype(BF16), axis, swap).astype(F32)
    out = total.astype(BF16)
    for step in range(half - 1):
        hops = [(half - 1 - step, half - 2 - step), (half + step, half + step + 1)]
        got = lax.ppermute(out, axis, hops)
        mine = (me == half - 2 - step) | (me == half + step + 1)
        out = jnp.where(mine, got, out)
    return out


def gather_on_line(block, axis, n):
    up = [(i, i + 1) for i in range(n - 1)]
    down = [(i + 1, i) for i in range(n - 1)]
    rights, lefts = [block], [block]
    for _ in range(n - 1):
        rights.append(lax.ppermute(rights[-1], axis, up))
        lefts.append(lax.ppermute(lefts[-1], axis, down))
    me = lax.axis_index(axis)
    slots = [block]
    for k in range(1, n):
        slots.append(jnp.where(me >= k, rights[k], lefts[n - k]))
    return slots


def make_body(n_out, n_inp, n_dp):
    def swap_dp(x):
        return lax.ppermute(x, "dp", [(0, 1), (1, 0)])

    def by_dp(mine, other):
        first = lax.axis_index("dp") == 0
        return jnp.concatenate([jnp.where(first, mine, other), jnp.where(first, other, mine)], axis=0)

    def in_order(slots, axis, n):
        me = lax.axis_index(axis)
        if n == 2:
            first = me == 0
            return [jnp.where(first, slots[0], slots[1]), jnp.where(first, slots[1], slots[0])]
        stacked = jnp.stack(slots)
        return [lax.dynamic_index_in_dim(stacked, lax.rem(me - j + n, n), 0, keepdims=False) for j in range(n)]

    def body(activations, out_grads, basis_in, basis_out):
        ex, tok, width = activations.shape
        grads = [out_grads]
        for k in range(1, n_inp):
            grads.append(lax.ppermute(out_grads, "inp", [(i, (i + k) % n_inp) for i in range(n_inp)]))
        acts = jnp.stack(gather_on_line(activations, "out", n_out))

        def project(block):
            block = lax.all_gather(block, "dp", axis=0, tiled=True)
            e, t, f = block.shape
            partial = jnp.dot(block.reshape(e * t, f), basis_out, preferred_element_type=F32)
            cuts = 4 if e % 4 == 0 and (e // 4) * t % 16 == 0 else 1
            rows = e * t // cuts
            parts = [lax.optimization_barrier(partial[c * rows:(c + 1) * rows]) for c in range(cuts)]
            sums = [sum_on_line(part, "out", n_out) for part in parts]
            return jnp.concatenate(sums, axis=0).reshape(e, t, -1)

        projected = [project(block) for block in grads]

        act_partial = jnp.dot(acts.reshape(n_out * ex * tok, width), basis_in, preferred_element_type=F32)
        total = act_partial
        sent = act_partial.astype(BF16)
        for k in range(1, n_inp):
            total = total + lax.ppermute(sent, "inp", [(i, (i + k) % n_inp) for i in range(n_inp)]).astype(F32)
        act_own = total.astype(BF16).reshape(n_out, ex, tok, -1)
        act_own = jnp.concatenate(in_order([act_own[k] for k in range(n_out)], "out", n_out), axis=1)
        count_rows = n_dp * act_own.shape[0] * act_own.shape[1]
        root = 1
        while root * root < count_rows:
            root *= 2
        scaled = root * root == count_rows
        if scaled:
            act_own = act_own * jnp.asarray(1.0 / root, BF16)
        act_hat = by_dp(act_own, swap_dp(act_own))

        grad_hat = jnp.concatenate(in_order(projected, "inp", n_inp), axis=1)

        rotated = jnp.einsum("etd,etf->edf", act_hat, grad_hat, preferred_element_type=F32)
        total = jnp.sum(rotated * rotated, axis=0)
        return total if scaled else total / count_rows

    return body


def solution(mesh):
    shape = dict(mesh.shape)
    placed = (
        P(("group", "dp"), "out", "inp"),
        P(("group", "dp"), "inp", "out"),
        P("inp", "out"),
        P("out", ("inp", "dp")),
    )
    return jax.shard_map(
        make_body(shape["out"], shape["inp"], shape["dp"]),
        mesh=mesh,
        in_specs=placed,
        out_specs=P(("group", "out"), ("inp", "dp")),
        check_vma=False,
    )
```
